32 devices in a mesh: dp: 4 (over y, x), vocab: 8 (over z, core).
Axes of the slice: x: 2, y: 2, z: 4, core: 2. Of those that a mesh axis runs over, the one named last changes fastest.
Arguments:
- hidden: bfloat16 [128, 3584], P(('dp', 'vocab')), may hold values from -6 to 6
- head_weight: bfloat16 [3584, 256000], P(None, ('dp', 'vocab')), may hold values from -0.75 to 0.75
- teacher_ids: int32 [128, 128], P(('dp', 'vocab')), may hold values from 0 to 255999
- teacher_probs: float32 [128, 128], P(('dp', 'vocab')), may hold values from 0.0001 to 0.015
- target_ids: int32 [128], P(('dp', 'vocab')), may hold values from 0 to 255999
Outputs:
- token_loss: float32 [128], P(('dp', 'vocab'))
- hidden_grad: bfloat16 [128, 3584], P(('dp', 'vocab'))
The draws below stay inside these ranges and needn't reach their ends.
All inputs are finite; a program needn't handle non-finite values.
Results may differ from the reference program's by a relative error of at most 0.004.
Values may be sent and summed in bfloat16 or wider, within the bound.
A program may use at most 128 MiB of HBM per device.

```python
import math
import jax
import jax.numpy as jnp
import numpy as np
from jax import lax

D = 3584
V = 256000
K = 128
TOKENS = 128


def plant(result, rng, least, top_value):
    longest = result.shape.index(max(result.shape))
    spots = []
    for shift in (0, 1):
        where = [jax.random.randint(jax.random.fold_in(rng, axis), (), 0, length) for axis, length in enumerate(result.shape)]
        where[longest] = (where[longest] + shift) % result.shape[longest]
        spots.append(tuple(where))
    return result.at[spots[0]].set(least).at[spots[1]].set(top_value)


def block_scale(rng, shape, shards, smallest, largest):
    level, own = 1.0, jax.random.fold_in(rng, 6)
    for position, parts in shards:
        draws = jnp.exp(jax.random.uniform(jax.random.fold_in(own, position), (parts,), jnp.float32, smallest / len(shards), largest / len(shards)))
        level = level * jnp.repeat(draws, shape[position] // parts).reshape([-1 if axis == position else 1 for axis in range(len(shape))])
    return level


def wide_ids(rng, extent, count, skew):
    weights = [min(1 << octave, count + 1 - (1 << octave)) * (1 << 20) // math.isqrt((1 << octave) ** skew) + 1 for octave in range((count + 1).bit_length()) if 1 << octave <= count]
    deviation = 1 + sum(weights) // (1 << 30)
    listing = np.cumsum(np.array([max(1, weight // deviation) for weight in weights]))
    pick = jax.random.randint(jax.random.fold_in(rng, 1), extent, 0, int(listing[len(weights) - 1]))
    start = jnp.left_shift(1, jnp.searchsorted(jnp.asarray(listing, jnp.int32), pick, side="right").astype(jnp.int32))
    grade = start - 1 + jax.random.randint(jax.random.fold_in(rng, 4), extent, 0, 1 << 30) % jnp.minimum(start, count + 1 - start)
    return jax.random.permutation(jax.random.fold_in(rng, 2), count)[grade].astype(jnp.int32)


def bell_draw(rng, shape, deviation, reach, shards=(), held_as=jnp.bfloat16):
    entries = deviation * jax.random.normal(rng, shape, jnp.float32)
    if shards:
        entries = entries * block_scale(rng, shape, shards, -0.22, 0.18)
    return jnp.clip(entries, -reach, reach).astype(held_as)


def setup_inputs(seed: int = 0) -> dict:
    keys = jax.random.split(jax.random.key(seed), 6)
    return {
        "hidden": bell_draw(keys[0], (TOKENS, D), 1.0, 6.0, ((0, 32),)),
        "head_weight": bell_draw(keys[1], (D, V), 64 ** -0.5, 0.75, ((1, 32),)),
        "teacher_ids": plant(wide_ids(keys[2], (TOKENS, K), V, 2), jax.random.fold_in(keys[2], 3), 0, V - 1).astype(jnp.int32),
        "teacher_probs": jnp.clip(jnp.exp(math.log(0.015) - 5.0106353 * jax.random.uniform(keys[3], (TOKENS, K), jnp.float32) ** block_scale(keys[3], (TOKENS, K), ((0, 32),), -0.2, 0.2)), 0.0001, 0.015),
        "target_ids": plant(jax.random.randint(keys[4], (TOKENS,), 0, V), jax.random.fold_in(keys[4], 1), 0, V - 1).astype(jnp.int32),
    }


SOFT_CAP = 30.0
CE_WEIGHT = 0.5
LOSS_SCALE = 8.0


def teacher_terms(capped, first_column, teacher_ids, teacher_probs, target_ids):
    slice_width = capped.shape[1]
    inside = (teacher_ids >= first_column) & (teacher_ids < first_column + slice_width)
    local_column = jnp.clip(teacher_ids - first_column, 0, slice_width - 1).astype(jnp.int32)
    picked = jnp.take_along_axis(capped, local_column, axis=1)
    teacher_dot = jnp.sum(jnp.where(inside, teacher_probs * picked, 0.0), axis=1)
    columns = first_column + jnp.arange(slice_width, dtype=jnp.int32)
    target_hit = columns[None, :] == target_ids[:, None]
    target_logit = jnp.sum(jnp.where(target_hit, capped, 0.0), axis=1)
    return inside, local_column, target_hit, teacher_dot, target_logit


def logit_grads(capped, log_total, teacher_sum, inside, local_column, teacher_probs, target_hit):
    token_count = capped.shape[0]
    row_index = jnp.broadcast_to(jnp.arange(token_count, dtype=jnp.int32)[:, None], local_column.shape)
    sparse = jnp.zeros(capped.shape, jnp.float32).at[row_index, local_column].add(jnp.where(inside, teacher_probs, 0.0))
    softmax_rows = jnp.exp(capped - log_total[:, None])
    onehot = jnp.where(target_hit, 1.0, 0.0)
    raw_grads = LOSS_SCALE * ((teacher_sum + CE_WEIGHT)[:, None] * softmax_rows - sparse - CE_WEIGHT * onehot)
    return (raw_grads * (1.0 - (capped / SOFT_CAP) ** 2)).astype(jnp.bfloat16)


def reference(hidden, head_weight, teacher_ids, teacher_probs, target_ids):
    blocks = 32
    slice_width = V // blocks
    token_count = hidden.shape[0]

    def capped_block(block_index):
        first_column = (block_index * slice_width).astype(jnp.int32)
        block = lax.dynamic_slice_in_dim(head_weight, first_column, slice_width, 1)
        raw_logits = jnp.dot(hidden, block, preferred_element_type=jnp.float32)
        return first_column, block, SOFT_CAP * jnp.tanh(raw_logits / SOFT_CAP)

    def block_stats(totals, block_index):
        first_column, block, capped = capped_block(block_index)
        terms = teacher_terms(capped, first_column, teacher_ids, teacher_probs, target_ids)
        exp_total = jnp.sum(jnp.exp(capped), axis=1)
        return (totals[0] + exp_total, totals[1] + terms[3], totals[2] + terms[4]), None

    zeros_rows = jnp.zeros((token_count,), jnp.float32)
    indices = jnp.arange(blocks, dtype=jnp.int32)
    (exp_sum, teacher_dot, target_logit), _ = lax.scan(block_stats, (zeros_rows, zeros_rows, zeros_rows), indices)
    log_total = jnp.log(exp_sum)
    teacher_sum = jnp.sum(teacher_probs, axis=1)
    token_loss = jnp.sum(teacher_probs * jnp.log(teacher_probs), axis=1) - teacher_dot + teacher_sum * log_total + CE_WEIGHT * (log_total - target_logit)

    def block_grads(accum, block_index):
        first_column, block, capped = capped_block(block_index)
        inside, local_column, target_hit, _, _ = teacher_terms(capped, first_column, teacher_ids, teacher_probs, target_ids)
        grads = logit_grads(capped, log_total, teacher_sum, inside, local_column, teacher_probs, target_hit)
        return accum + jnp.einsum("tv,dv->td", grads, block, preferred_element_type=jnp.float32), None

    accum, _ = lax.scan(block_grads, jnp.zeros((token_count, D), jnp.float32), indices)
    return token_loss, accum.astype(jnp.bfloat16)
```

```python
import functools
import jax
import jax.numpy as jnp
from jax import lax
from jax.experimental import pallas as pl
from jax.experimental.pallas import tpu as pltpu
from jax.sharding import PartitionSpec as P

SOFT_CAP = 30.0
CE_WEIGHT = 0.5
LOSS_SCALE = 8.0
BLOCK = 512
LANES = 128
ROW_CHUNK = 512
AXES = ("dp", "vocab")
NT = (((1,), (1,)), ((), ()))


def head_kernel(width, hidden_ref, w_ref, ids_ref, hi_probs_ref, lo_probs_ref, targets_ref,
                acc_ref, stats_ref, sparse_ref):
    step = pl.program_id(0)
    steps = pl.num_programs(0)
    tokens, depth = hidden_ref.shape
    kept = ids_ref.shape[1]
    groups = sparse_ref.shape[0]
    group_rows = 16 * pl.cdiv(groups, 16)

    @pl.when(step == 0)
    def _():
        acc_ref[...] = jnp.zeros_like(acc_ref)
        stats_ref[...] = jnp.zeros_like(stats_ref)
        group_row = lax.broadcasted_iota(jnp.int32, (group_rows, kept), 0)
        lane_row = lax.broadcasted_iota(jnp.int32, (LANES, kept), 0)

        def one_token(t, carry):
            ids = ids_ref[pl.ds(t, 1), :]
            high = jnp.where(group_row == (ids >> 7), 1.0, 0.0).astype(jnp.bfloat16)
            same = lane_row == (ids & 127)
            first = jnp.where(same, hi_probs_ref[pl.ds(t, 1), :], 0.0).astype(jnp.bfloat16)
            second = jnp.where(same, lo_probs_ref[pl.ds(t, 1), :], 0.0).astype(jnp.bfloat16)
            rows = lax.dot_general(
                jnp.concatenate([high, high], axis=1),
                jnp.concatenate([first, second], axis=1),
                NT, preferred_element_type=jnp.float32)
            sparse_ref[:, pl.ds(t, 1), :] = rows[:groups].reshape(groups, 1, LANES)
            return carry

        lax.fori_loop(0, tokens, one_token, 0, unroll=8)

    def block(columns, valid, w):
        logits = jnp.dot(hidden_ref[...], w(0, depth), preferred_element_type=jnp.float32)
        ratio = jnp.tanh(logits * (1.0 / SOFT_CAP))
        capped = SOFT_CAP * ratio
        slope = 1.0 - ratio * ratio
        lane = lax.broadcasted_iota(jnp.int32, (tokens, columns), 1)
        exps = jnp.exp(capped)
        sparse = jnp.concatenate(
            [sparse_ref[step * (BLOCK // LANES) + i] for i in range(columns // LANES)], axis=1)
        sparse = sparse + jnp.where(lane + step * BLOCK == targets_ref[...], CE_WEIGHT, 0.0)
        if valid != columns:
            inside = lane < valid
            exps = jnp.where(inside, exps, 0.0)
            sparse = jnp.where(inside, sparse, 0.0)
        stats_ref[:, 0:1] += jnp.sum(exps, axis=1, keepdims=True)
        stats_ref[:, 1:2] += jnp.sum(capped * sparse, axis=1, keepdims=True)
        grads = jnp.concatenate([exps * slope, sparse * slope], axis=0).astype(jnp.bfloat16)

        def chunk(i, carry):
            rows = pl.ds(pl.multiple_of(i * ROW_CHUNK, ROW_CHUNK), ROW_CHUNK)
            acc_ref[:, rows] += lax.dot_general(
                grads, w(i * ROW_CHUNK, ROW_CHUNK), NT, preferred_element_type=jnp.float32)
            return carry

        for i in range(depth // ROW_CHUNK):
            chunk(i, 0)

    last = width - (pl.cdiv(width, BLOCK) - 1) * BLOCK
    last_columns = LANES * pl.cdiv(last, LANES)

    @pl.when(step < steps - 1)
    def _():
        block(BLOCK, BLOCK, lambda start, size: w_ref[pl.ds(start, size), :])

    @pl.when(step == steps - 1)
    def _():
        def masked(start, size):
            piece = w_ref[pl.ds(start, size), :last_columns]
            lane = lax.broadcasted_iota(jnp.int32, piece.shape, 1)
            return jnp.where(lane < last, piece, jnp.zeros_like(piece))

        block(last_columns, last, masked)


def head_pass(hidden, head_weight, local_ids, probs, local_targets):
    tokens, depth = hidden.shape
    width = head_weight.shape[1]
    kept = local_ids.shape[1]
    groups = pl.cdiv(width, LANES)
    hi_probs = probs.astype(jnp.bfloat16).astype(jnp.float32)
    lo_probs = probs - hi_probs
    full = lambda shape: pl.BlockSpec(shape, lambda j: (0, 0), pipeline_mode=pl.Buffered(1))
    return pl.pallas_call(
        functools.partial(head_kernel, width),
        grid=(pl.cdiv(width, BLOCK),),
        in_specs=[
            full((tokens, depth)),
            pl.BlockSpec((depth, BLOCK), lambda j: (0, j)),
            full((tokens, kept)),
            full((tokens, kept)),
            full((tokens, kept)),
            full((tokens, 1)),
        ],
        out_specs=[full((2 * tokens, depth)), full((tokens, LANES))],
        out_shape=[
            jax.ShapeDtypeStruct((2 * tokens, depth), jnp.float32),
            jax.ShapeDtypeStruct((tokens, LANES), jnp.float32),
        ],
        scratch_shapes=[pltpu.VMEM((groups, tokens, LANES), jnp.float32)],
        compiler_params=pltpu.CompilerParams(vmem_limit_bytes=58 * 1024 * 1024),
        cost_estimate=pl.CostEstimate(
            flops=6 * tokens * depth * width, bytes_accessed=2 * depth * width,
            transcendentals=2 * tokens * width),
        name="head_pass",
    )(hidden, head_weight, local_ids, hi_probs, lo_probs, local_targets[:, None])


def per_device(hidden, head_weight, teacher_ids, teacher_probs, target_ids):
    width = head_weight.shape[1]
    tokens_local = hidden.shape[0]
    position = lax.axis_index(AXES)
    first_column = position * width
    gather = lambda x: lax.all_gather(x, AXES, axis=0, tiled=True)
    all_hidden = gather(hidden)
    all_ids = gather(jnp.concatenate([teacher_ids, target_ids[:, None]], axis=1))
    all_probs = gather(teacher_probs)
    kept = teacher_ids.shape[1]
    local = all_ids - first_column
    acc, stats = head_pass(all_hidden, head_weight, local[:, :kept], all_probs, local[:, kept])
    tokens = all_hidden.shape[0]
    totals = lax.psum(stats[:, :2], AXES)
    exp_sum, dots = totals[:, 0], totals[:, 1]
    teacher_sum = jnp.sum(all_probs, axis=1)
    scale = LOSS_SCALE * (teacher_sum + CE_WEIGHT) / exp_sum
    part = scale[:, None] * acc[:tokens] - LOSS_SCALE * acc[tokens:]
    summed = lax.psum_scatter(part, AXES, scatter_dimension=0, tiled=True)
    own = lambda x: lax.dynamic_slice_in_dim(x, position * tokens_local, tokens_local)
    own_sum = jnp.sum(teacher_probs, axis=1)
    loss = (
        jnp.sum(teacher_probs * jnp.log(teacher_probs), axis=1)
        - own(dots)
        + (own_sum + CE_WEIGHT) * jnp.log(own(exp_sum))
    )
    return loss, summed.astype(jnp.bfloat16)


def solution(mesh):
    in_specs = (
        P(AXES, None),
        P(None, AXES),
        P(AXES, None),
        P(AXES, None),
        P(AXES),
    )
    out_specs = (P(AXES), P(AXES, None))
    return jax.shard_map(
        per_device, mesh=mesh, in_specs=in_specs, out_specs=out_specs, check_vma=False
    )
```

```python
import functools
import jax
import jax.numpy as jnp
from jax import lax
from jax.experimental import pallas as pl
from jax.experimental.pallas import tpu as pltpu
from jax.sharding import PartitionSpec as P

SOFT_CAP = 30.0
CE_WEIGHT = 0.5
LOSS_SCALE = 8.0
BLOCK = 512
LANES = 128
ROW_CHUNK = 512
AXES = ("dp", "vocab")
MESH = pl.DeviceIdType.MESH
NT = (((1,), (1,)), ((), ()))


def head_kernel(width, hidden_ref, w_ref, ids_ref, hi_probs_ref, lo_probs_ref, targets_ref,
                acc_ref, stats_ref, sparse_ref):
    step = pl.program_id(0)
    steps = pl.num_programs(0)
    tokens, depth = hidden_ref.shape
    kept = ids_ref.shape[1]
    groups = sparse_ref.shape[0]
    group_rows = 16 * pl.cdiv(groups, 16)

    @pl.when(step == 0)
    def _():
        acc_ref[...] = jnp.zeros_like(acc_ref)
        stats_ref[...] = jnp.zeros_like(stats_ref)
        group_row = lax.broadcasted_iota(jnp.int32, (group_rows, kept), 0)
        lane_row = lax.broadcasted_iota(jnp.int32, (LANES, kept), 0)

        def one_token(t, carry):
            ids = ids_ref[pl.ds(t, 1), :]
            high = jnp.where(group_row == (ids >> 7), 1.0, 0.0).astype(jnp.bfloat16)
            same = lane_row == (ids & 127)
            first = jnp.where(same, hi_probs_ref[pl.ds(t, 1), :], 0.0).astype(jnp.bfloat16)
            second = jnp.where(same, lo_probs_ref[pl.ds(t, 1), :], 0.0).astype(jnp.bfloat16)
            rows = lax.dot_general(
                jnp.concatenate([high, high], axis=1),
                jnp.concatenate([first, second], axis=1),
                NT, preferred_element_type=jnp.float32)
            sparse_ref[:, pl.ds(t, 1), :] = rows[:groups].reshape(groups, 1, LANES)
            return carry

        lax.fori_loop(0, tokens, one_token, 0, unroll=8)

    def block(columns):
        w = w_ref.at[pl.ds(0, columns)]
        logits = lax.dot_general(hidden_ref[...], w[...], NT, preferred_element_type=jnp.float32)
        ratio = jnp.tanh(logits * (1.0 / SOFT_CAP))
        capped = SOFT_CAP * ratio
        slope = 1.0 - ratio * ratio
        lane = lax.broadcasted_iota(jnp.int32, (tokens, columns), 1)
        exps = jnp.exp(capped)
        sparse = jnp.concatenate(
            [sparse_ref[step * (BLOCK // LANES) + i] for i in range(pl.cdiv(columns, LANES))],
            axis=1)[:, :columns]
        sparse = sparse + jnp.where(lane + step * BLOCK == targets_ref[...], CE_WEIGHT, 0.0)
        stats_ref[:, 0:1] += jnp.sum(exps, axis=1, keepdims=True)
        stats_ref[:, 1:2] += jnp.sum(capped * sparse, axis=1, keepdims=True)
        grads = jnp.concatenate([exps * slope, sparse * slope], axis=0).astype(jnp.bfloat16)
        for start in range(0, depth, ROW_CHUNK):
            part = slice(start, start + ROW_CHUNK)
            acc_ref[:, part] += jnp.dot(grads, w[:, part], preferred_element_type=jnp.float32)

    last = width - (pl.cdiv(width, BLOCK) - 1) * BLOCK

    @pl.when(step < steps - 1)
    def _():
        block(BLOCK)

    @pl.when(step == steps - 1)
    def _():
        block(last)


def head_pass(hidden, head_weight, local_ids, probs, local_targets):
    tokens, depth = hidden.shape
    width = head_weight.shape[1]
    kept = local_ids.shape[1]
    groups = pl.cdiv(width, LANES)
    hi_probs = probs.astype(jnp.bfloat16).astype(jnp.float32)
    lo_probs = probs - hi_probs
    full = lambda shape: pl.BlockSpec(shape, lambda j: (0, 0), pipeline_mode=pl.Buffered(1))
    return pl.pallas_call(
        functools.partial(head_kernel, width),
        grid=(pl.cdiv(width, BLOCK),),
        in_specs=[
            full((tokens, depth)),
            pl.BlockSpec((BLOCK, depth), lambda j: (j, 0)),
            full((tokens, kept)),
            full((tokens, kept)),
            full((tokens, kept)),
            full((tokens, 1)),
        ],
        out_specs=[full((2 * tokens, depth)), full((tokens, LANES))],
        out_shape=[
            jax.ShapeDtypeStruct((2 * tokens, depth), jnp.float32),
            jax.ShapeDtypeStruct((tokens, LANES), jnp.float32),
        ],
        scratch_shapes=[pltpu.VMEM((groups, tokens, LANES), jnp.float32)],
        compiler_params=pltpu.CompilerParams(vmem_limit_bytes=58 * 1024 * 1024),
        cost_estimate=pl.CostEstimate(
            flops=6 * tokens * depth * width, bytes_accessed=2 * depth * width,
            transcendentals=2 * tokens * width),
        name="head_pass",
    )(hidden, head_weight.T, local_ids, hi_probs, lo_probs, local_targets[:, None])


def meet(nd, nv):
    d, v = lax.axis_index("dp"), lax.axis_index("vocab")
    barrier = pltpu.get_barrier_semaphore()
    peers_v = [(d, lax.rem(v + o, nv)) for o in range(1, nv)]
    peers_d = [(lax.rem(d + o, nd), v) for o in range(1, nd)]
    for peer in peers_v + peers_d:
        pl.semaphore_signal(barrier, inc=1, device_id=peer, device_id_type=MESH)
    pl.semaphore_wait(barrier, nv + nd - 2)
    return d, v, peers_d, peers_v


def remote(src, dst, send, recv, peer):
    return pltpu.make_async_remote_copy(
        src_ref=src, dst_ref=dst, send_sem=send, recv_sem=recv,
        device_id=peer, device_id_type=MESH)


def gather_kernel(nd, nv, *refs):
    ins, outs = refs[:3], refs[3:6]
    send_v, recv_v, send_d, recv_d = refs[6:]
    d, v, peers_d, peers_v = meet(nd, nv)
    for i in range(3):
        outs[i][d * nv + v] = ins[i][...]
    copies = []
    for o, peer in enumerate(peers_v):
        for i in range(3):
            copy = remote(ins[i], outs[i].at[d * nv + v], send_v.at[i, o], recv_v.at[i, v], peer)
            copy.start()
            copies.append(copy)
    for o, peer in enumerate(peers_v):
        for i in range(3):
            source = peer[1]
            remote(ins[i], outs[i].at[d * nv + source], send_v.at[i, o],
                   recv_v.at[i, source], peer).wait_recv()
    for o, peer in enumerate(peers_d):
        for i in range(3):
            rows = outs[i].at[pl.ds(d * nv, nv)]
            copy = remote(rows, rows, send_d.at[i, o], recv_d.at[i, d], peer)
            copy.start()
            copies.append(copy)
    for o, peer in enumerate(peers_d):
        for i in range(3):
            rows = outs[i].at[pl.ds(peer[0] * nv, nv)]
            remote(rows, rows, send_d.at[i, o], recv_d.at[i, peer[0]], peer).wait_recv()
    for copy in copies:
        copy.wait_send()


def totals_kernel(nd, nv, in_ref, out_ref, slots_v, slots_d, held, send_v, recv_v, send_d, recv_d):
    d, v, peers_d, peers_v = meet(nd, nv)
    copies = []
    for peers, me, src, slots, send, recv, axis, result in (
        (peers_v, v, in_ref, slots_v, send_v, recv_v, 1, held),
        (peers_d, d, held, slots_d, send_d, recv_d, 0, out_ref),
    ):
        for o, peer in enumerate(peers):
            copy = remote(src, slots.at[me], send.at[o], recv.at[me], peer)
            copy.start()
            copies.append(copy)
        slots[me] = src[...]
        for o, peer in enumerate(peers):
            source = peer[axis]
            remote(src, slots.at[source], send.at[o], recv.at[source], peer).wait_recv()
        result[...] = jnp.sum(slots[...], axis=0)
    for copy in copies:
        copy.wait_send()


def reduce_kernel(nd, nv, in_ref, out_ref, slots_d, slots_v, held, send_d, recv_d, send_v, recv_v):
    d, v, peers_d, peers_v = meet(nd, nv)
    copies = []
    for o, peer in enumerate(peers_d):
        copy = remote(in_ref.at[peer[0]], slots_d.at[d], send_d.at[o], recv_d.at[d], peer)
        copy.start()
        copies.append(copy)
    held[...] = in_ref[d].astype(jnp.float32)
    for o, peer in enumerate(peers_d):
        source = peer[0]
        remote(in_ref.at[d], slots_d.at[source], send_d.at[o], recv_d.at[source], peer).wait_recv()
        held[...] += slots_d[source].astype(jnp.float32)
    for o, peer in enumerate(peers_v):
        copy = remote(held.at[peer[1]], slots_v.at[v], send_v.at[o], recv_v.at[v], peer)
        copy.start()
        copies.append(copy)
    total = held[v]
    for o, peer in enumerate(peers_v):
        source = peer[1]
        remote(held.at[v], slots_v.at[source], send_v.at[o], recv_v.at[source], peer).wait_recv()
        total = total + slots_v[source]
    out_ref[...] = total.astype(out_ref.dtype)
    for copy in copies:
        copy.wait_send()


def comm_call(kernel, number, name, args, out_shape, scratch):
    vmem = pl.BlockSpec(memory_space=pltpu.VMEM)
    return pl.pallas_call(
        kernel,
        out_shape=out_shape,
        in_specs=[vmem] * len(args),
        out_specs=[vmem] * len(out_shape),
        scratch_shapes=scratch,
        compiler_params=pltpu.CompilerParams(
            collective_id=number, has_side_effects=True, vmem_limit_bytes=48 * 1024 * 1024),
        name=name,
    )(*args)


def per_device(nd, nv, hidden, head_weight, teacher_ids, teacher_probs, target_ids):
    width = head_weight.shape[1]
    local_tokens, kept = teacher_ids.shape
    depth = hidden.shape[1]
    count = nd * nv
    tokens = count * local_tokens
    position = lax.axis_index(AXES)
    sems = lambda *shape: pltpu.SemaphoreType.DMA(shape)
    rows = local_tokens * depth // LANES
    pad = 8 * pl.cdiv(local_tokens + 1, 8)
    target_row = jnp.pad(target_ids, (0, kept - local_tokens))[None, :]
    ids = jnp.pad(jnp.concatenate([teacher_ids, target_row], axis=0),
                  ((0, pad - local_tokens - 1), (0, 0)))
    probs = jnp.pad(teacher_probs, ((0, pad - local_tokens), (0, 0)))
    args = (hidden.reshape(rows, LANES), ids, probs)
    got = comm_call(
        functools.partial(gather_kernel, nd, nv), 0, "gather_inputs", args,
        [jax.ShapeDtypeStruct((count,) + a.shape, a.dtype) for a in args],
        [sems(3, nv), sems(3, nv), sems(3, nd), sems(3, nd)])
    all_hidden = got[0].reshape(tokens, depth)
    local = got[1] - position * width
    local_ids = local[:, :local_tokens].reshape(tokens, kept)
    local_targets = local[:, local_tokens, :local_tokens].reshape(tokens)
    all_probs = got[2][:, :local_tokens].reshape(tokens, kept)
    acc, stats = head_pass(all_hidden, head_weight, local_ids, all_probs, local_targets)
    block = (8, tokens)
    totals = comm_call(
        functools.partial(totals_kernel, nd, nv), 1, "sum_stats", (stats[:, :8].T,),
        [jax.ShapeDtypeStruct(block, jnp.float32)],
        [pltpu.VMEM((nv,) + block, jnp.float32), pltpu.VMEM((nd,) + block, jnp.float32),
         pltpu.VMEM(block, jnp.float32), sems(nv), sems(nv), sems(nd), sems(nd)])[0]
    exp_sum, dots = totals[0], totals[1]
    teacher_sum = jnp.sum(all_probs, axis=1)
    scale = LOSS_SCALE * (teacher_sum + CE_WEIGHT) / exp_sum
    part = (scale[:, None] * acc[:tokens] - LOSS_SCALE * acc[tokens:]).astype(jnp.bfloat16)
    piece = (rows, LANES)
    grad = comm_call(
        functools.partial(reduce_kernel, nd, nv), 2, "sum_grads",
        (part.reshape((nd, nv) + piece),),
        [jax.ShapeDtypeStruct(piece, jnp.bfloat16)],
        [pltpu.VMEM((nd, nv) + piece, jnp.bfloat16), pltpu.VMEM((nv,) + piece, jnp.float32),
         pltpu.VMEM((nv,) + piece, jnp.float32), sems(nd), sems(nd), sems(nv), sems(nv)])[0]
    own = lambda x: lax.dynamic_slice_in_dim(x, position * local_tokens, local_tokens)
    own_sum = jnp.sum(teacher_probs, axis=1)
    loss = (
        jnp.sum(teacher_probs * jnp.log(teacher_probs), axis=1)
        - own(dots)
        + (own_sum + CE_WEIGHT) * jnp.log(own(exp_sum))
    )
    return loss, grad.reshape(local_tokens, depth)


def solution(mesh):
    in_specs = (
        P(AXES, None),
        P(None, AXES),
        P(AXES, None),
        P(AXES, None),
        P(AXES),
    )
    out_specs = (P(AXES), P(AXES, None))
    return jax.shard_map(
        functools.partial(per_device, mesh.shape["dp"], mesh.shape["vocab"]),
        mesh=mesh, in_specs=in_specs, out_specs=out_specs, check_vma=False
    )
```

```python
import functools
import jax
import jax.numpy as jnp
from jax import lax
from jax.experimental import pallas as pl
from jax.experimental.pallas import tpu as pltpu
from jax.sharding import PartitionSpec as P

SOFT_CAP = 30.0
CE_WEIGHT = 0.5
LOSS_SCALE = 8.0
BLOCK = 512
LANES = 128
ROW_CHUNK = 512
AXES = ("dp", "vocab")
MESH = pl.DeviceIdType.MESH
NT = (((1,), (1,)), ((), ()))


def head_kernel(width, hidden_ref, w_ref, ids_ref, hi_probs_ref, lo_probs_ref, targets_ref,
                acc_ref, stats_ref, sparse_ref):
    step = pl.program_id(0)
    steps = pl.num_programs(0)
    depth, tokens = hidden_ref.shape
    kept = ids_ref.shape[1]
    groups = sparse_ref.shape[0]
    group_rows = 16 * pl.cdiv(groups, 16)

    @pl.when(step == 0)
    def _():
        acc_ref[...] = jnp.zeros_like(acc_ref)
        stats_ref[...] = jnp.zeros_like(stats_ref)
        group_row = lax.broadcasted_iota(jnp.int32, (group_rows, kept), 0)
        lane_row = lax.broadcasted_iota(jnp.int32, (LANES, kept), 0)

        def one_token(t, carry):
            ids = ids_ref[pl.ds(t, 1), :]
            high = jnp.where(group_row == (ids >> 7), 1.0, 0.0).astype(jnp.bfloat16)
            same = lane_row == (ids & 127)
            first = jnp.where(same, hi_probs_ref[pl.ds(t, 1), :], 0.0).astype(jnp.bfloat16)
            second = jnp.where(same, lo_probs_ref[pl.ds(t, 1), :], 0.0).astype(jnp.bfloat16)
            rows = lax.dot_general(
                jnp.concatenate([high, high], axis=1),
                jnp.concatenate([first, second], axis=1),
                NT, preferred_element_type=jnp.float32)
            sparse_ref[:, pl.ds(t, 1), :] = rows[:groups].reshape(groups, 1, LANES)
            return carry

        lax.fori_loop(0, tokens, one_token, 0, unroll=8)

    def block(columns):
        w = w_ref.at[pl.ds(0, columns)]
        logits = jnp.dot(w[...], hidden_ref[...], preferred_element_type=jnp.float32).T
        ratio = jnp.tanh(logits * (1.0 / SOFT_CAP))
        capped = SOFT_CAP * ratio
        slope = 1.0 - ratio * ratio
        lane = lax.broadcasted_iota(jnp.int32, (tokens, columns), 1)
        exps = jnp.exp(capped)
        sparse = jnp.concatenate(
            [sparse_ref[step * (BLOCK // LANES) + i] for i in range(pl.cdiv(columns, LANES))],
            axis=1)[:, :columns]
        sparse = sparse + jnp.where(lane + step * BLOCK == targets_ref[...], CE_WEIGHT, 0.0)
        stats_ref[:, 0:1] += jnp.sum(exps, axis=1, keepdims=True)
        stats_ref[:, 1:2] += jnp.sum(capped * sparse, axis=1, keepdims=True)
        grads = jnp.concatenate([exps * slope, sparse * slope], axis=0).astype(jnp.bfloat16)
        for start in range(0, depth, ROW_CHUNK):
            part = slice(start, start + ROW_CHUNK)
            acc_ref[:, part] += jnp.dot(grads, w[:, part], preferred_element_type=jnp.float32)

    last = width - (pl.cdiv(width, BLOCK) - 1) * BLOCK

    @pl.when(step < steps - 1)
    def _():
        block(BLOCK)

    @pl.when(step == steps - 1)
    def _():
        block(last)


def head_pass(hidden, head_weight, local_ids, probs, local_targets):
    tokens, depth = hidden.shape
    width = head_weight.shape[1]
    kept = local_ids.shape[1]
    groups = pl.cdiv(width, LANES)
    hi_probs = probs.astype(jnp.bfloat16).astype(jnp.float32)
    lo_probs = probs - hi_probs
    full = lambda shape: pl.BlockSpec(shape, lambda j: (0, 0), pipeline_mode=pl.Buffered(1))
    return pl.pallas_call(
        functools.partial(head_kernel, width),
        grid=(pl.cdiv(width, BLOCK),),
        in_specs=[
            full((depth, tokens)),
            pl.BlockSpec((BLOCK, depth), lambda j: (j, 0)),
            full((tokens, kept)),
            full((tokens, kept)),
            full((tokens, kept)),
            full((tokens, 1)),
        ],
        out_specs=[full((2 * tokens, depth)), full((tokens, LANES))],
        out_shape=[
            jax.ShapeDtypeStruct((2 * tokens, depth), jnp.float32),
            jax.ShapeDtypeStruct((tokens, LANES), jnp.float32),
        ],
        scratch_shapes=[pltpu.VMEM((groups, tokens, LANES), jnp.float32)],
        compiler_params=pltpu.CompilerParams(vmem_limit_bytes=58 * 1024 * 1024),
        cost_estimate=pl.CostEstimate(
            flops=6 * tokens * depth * width, bytes_accessed=2 * depth * width,
            transcendentals=2 * tokens * width),
        name="head_pass",
    )(hidden.T, head_weight.T, local_ids, hi_probs, lo_probs, local_targets[:, None])


def meet(nd, nv):
    d, v = lax.axis_index("dp"), lax.axis_index("vocab")
    barrier = pltpu.get_barrier_semaphore()
    peers_v = [(d, lax.rem(v + o, nv)) for o in range(1, nv)]
    peers_d = [(lax.rem(d + o, nd), v) for o in range(1, nd)]
    for peer in peers_v + peers_d:
        pl.semaphore_signal(barrier, inc=1, device_id=peer, device_id_type=MESH)
    pl.semaphore_wait(barrier, nv + nd - 2)
    return d, v, peers_d, peers_v


def remote(src, dst, send, recv, peer):
    return pltpu.make_async_remote_copy(
        src_ref=src, dst_ref=dst, send_sem=send, recv_sem=recv,
        device_id=peer, device_id_type=MESH)


def gather_kernel(nd, nv, *refs):
    ins, outs = refs[:3], refs[3:6]
    send_v, recv_v, send_d, recv_d = refs[6:]
    d, v, peers_d, peers_v = meet(nd, nv)
    for i in range(3):
        outs[i][d * nv + v] = ins[i][...]
    copies = []
    for o, peer in enumerate(peers_v):
        for i in range(3):
            copy = remote(ins[i], outs[i].at[d * nv + v], send_v.at[i, o], recv_v.at[i, v], peer)
            copy.start()
            copies.append(copy)
    for o, peer in enumerate(peers_v):
        for i in range(3):
            source = peer[1]
            remote(ins[i], outs[i].at[d * nv + source], send_v.at[i, o],
                   recv_v.at[i, source], peer).wait_recv()
    for o, peer in enumerate(peers_d):
        for i in range(3):
            rows = outs[i].at[pl.ds(d * nv, nv)]
            copy = remote(rows, rows, send_d.at[i, o], recv_d.at[i, d], peer)
            copy.start()
            copies.append(copy)
    for o, peer in enumerate(peers_d):
        for i in range(3):
            rows = outs[i].at[pl.ds(peer[0] * nv, nv)]
            remote(rows, rows, send_d.at[i, o], recv_d.at[i, peer[0]], peer).wait_recv()
    for copy in copies:
        copy.wait_send()


def totals_kernel(nd, nv, in_ref, out_ref, slots_v, slots_d, held, send_v, recv_v, send_d, recv_d):
    d, v, peers_d, peers_v = meet(nd, nv)
    copies = []
    for peers, me, src, slots, send, recv, axis, result in (
        (peers_v, v, in_ref, slots_v, send_v, recv_v, 1, held),
        (peers_d, d, held, slots_d, send_d, recv_d, 0, out_ref),
    ):
        for o, peer in enumerate(peers):
            copy = remote(src, slots.at[me], send.at[o], recv.at[me], peer)
            copy.start()
            copies.append(copy)
        slots[me] = src[...]
        for o, peer in enumerate(peers):
            source = peer[axis]
            remote(src, slots.at[source], send.at[o], recv.at[source], peer).wait_recv()
        result[...] = jnp.sum(slots[...], axis=0)
    for copy in copies:
        copy.wait_send()


def reduce_kernel(nd, nv, in_ref, out_ref, slots_d, slots_v, held, send_d, recv_d, send_v, recv_v):
    d, v, peers_d, peers_v = meet(nd, nv)
    copies = []
    for o, peer in enumerate(peers_d):
        copy = remote(in_ref.at[peer[0]], slots_d.at[d], send_d.at[o], recv_d.at[d], peer)
        copy.start()
        copies.append(copy)
    held[...] = in_ref[d].astype(jnp.float32)
    for o, peer in enumerate(peers_d):
        source = peer[0]
        remote(in_ref.at[d], slots_d.at[source], send_d.at[o], recv_d.at[source], peer).wait_recv()
        held[...] += slots_d[source].astype(jnp.float32)
    for o, peer in enumerate(peers_v):
        copy = remote(held.at[peer[1]], slots_v.at[v], send_v.at[o], recv_v.at[v], peer)
        copy.start()
        copies.append(copy)
    total = held[v]
    for o, peer in enumerate(peers_v):
        source = peer[1]
        remote(held.at[v], slots_v.at[source], send_v.at[o], recv_v.at[source], peer).wait_recv()
        total = total + slots_v[source]
    out_ref[...] = total.astype(out_ref.dtype)
    for copy in copies:
        copy.wait_send()


def comm_call(kernel, number, name, args, out_shape, scratch):
    vmem = pl.BlockSpec(memory_space=pltpu.VMEM)
    return pl.pallas_call(
        kernel,
        out_shape=out_shape,
        in_specs=[vmem] * len(args),
        out_specs=[vmem] * len(out_shape),
        scratch_shapes=scratch,
        compiler_params=pltpu.CompilerParams(
            collective_id=number, has_side_effects=True, vmem_limit_bytes=48 * 1024 * 1024),
        name=name,
    )(*args)


def per_device(nd, nv, hidden, head_weight, teacher_ids, teacher_probs, target_ids):
    width = head_weight.shape[1]
    local_tokens, kept = teacher_ids.shape
    depth = hidden.shape[1]
    count = nd * nv
    tokens = count * local_tokens
    position = lax.axis_index(AXES)
    sems = lambda *shape: pltpu.SemaphoreType.DMA(shape)
    rows = local_tokens * depth // LANES
    pad = 8 * pl.cdiv(local_tokens + 1, 8)
    target_row = jnp.pad(target_ids, (0, kept - local_tokens))[None, :]
    ids = jnp.pad(jnp.concatenate([teacher_ids, target_row], axis=0),
                  ((0, pad - local_tokens - 1), (0, 0)))
    probs = jnp.pad(teacher_probs, ((0, pad - local_tokens), (0, 0)))
    args = (hidden.reshape(rows, LANES), ids, probs)
    got = comm_call(
        functools.partial(gather_kernel, nd, nv), 0, "gather_inputs", args,
        [jax.ShapeDtypeStruct((count,) + a.shape, a.dtype) for a in args],
        [sems(3, nv), sems(3, nv), sems(3, nd), sems(3, nd)])
    all_hidden = got[0].reshape(tokens, depth)
    local = got[1] - position * width
    local_ids = local[:, :local_tokens].reshape(tokens, kept)
    local_targets = local[:, local_tokens, :local_tokens].reshape(tokens)
    all_probs = got[2][:, :local_tokens].reshape(tokens, kept)
    acc, stats = head_pass(all_hidden, head_weight, local_ids, all_probs, local_targets)
    block = (8, tokens)
    totals = comm_call(
        functools.partial(totals_kernel, nd, nv), 1, "sum_stats", (stats[:, :8].T,),
        [jax.ShapeDtypeStruct(block, jnp.float32)],
        [pltpu.VMEM((nv,) + block, jnp.float32), pltpu.VMEM((nd,) + block, jnp.float32),
         pltpu.VMEM(block, jnp.float32), sems(nv), sems(nv), sems(nd), sems(nd)])[0]
    exp_sum, dots = totals[0], totals[1]
    teacher_sum = jnp.sum(all_probs, axis=1)
    scale = LOSS_SCALE * (teacher_sum + CE_WEIGHT) / exp_sum
    part = (scale[:, None] * acc[:tokens] - LOSS_SCALE * acc[tokens:]).astype(jnp.bfloat16)
    piece = (rows, LANES)
    grad = comm_call(
        functools.partial(reduce_kernel, nd, nv), 2, "sum_grads",
        (part.reshape((nd, nv) + piece),),
        [jax.ShapeDtypeStruct(piece, jnp.bfloat16)],
        [pltpu.VMEM((nd, nv) + piece, jnp.bfloat16), pltpu.VMEM((nv,) + piece, jnp.float32),
         pltpu.VMEM((nv,) + piece, jnp.float32), sems(nd), sems(nd), sems(nv), sems(nv)])[0]
    own = lambda x: lax.dynamic_slice_in_dim(x, position * local_tokens, local_tokens)
    own_sum = jnp.sum(teacher_probs, axis=1)
    loss = (
        jnp.sum(teacher_probs * jnp.log(teacher_probs), axis=1)
        - own(dots)
        + (own_sum + CE_WEIGHT) * jnp.log(own(exp_sum))
    )
    return loss, grad.reshape(local_tokens, depth)


def solution(mesh):
    in_specs = (
        P(AXES, None),
        P(None, AXES),
        P(AXES, None),
        P(AXES, None),
        P(AXES),
    )
    out_specs = (P(AXES), P(AXES, None))
    return jax.shard_map(
        functools.partial(per_device, mesh.shape["dp"], mesh.shape["vocab"]),
        mesh=mesh, in_specs=in_specs, out_specs=out_specs, check_vma=False
    )
```

```python
import functools
import jax
import jax.numpy as jnp
from jax import lax
from jax.experimental import pallas as pl
from jax.experimental.pallas import tpu as pltpu
from jax.sharding import PartitionSpec as P

SOFT_CAP = 30.0
CE_WEIGHT = 0.5
LOSS_SCALE = 8.0
BLOCK = 1024
LANES = 128
ROW_CHUNK = 512
AXES = ("dp", "vocab")
MESH = pl.DeviceIdType.MESH
NT = (((1,), (1,)), ((), ()))


def head_kernel(width, hidden_ref, w_ref, ids_ref, hi_probs_ref, lo_probs_ref, targets_ref,
                acc_ref, stats_ref, sparse_ref):
    step = pl.program_id(0)
    steps = pl.num_programs(0)
    tokens, depth = hidden_ref.shape
    kept = ids_ref.shape[1]
    groups = sparse_ref.shape[0]
    group_rows = 16 * pl.cdiv(groups, 16)

    @pl.when(step == 0)
    def _():
        acc_ref[...] = jnp.zeros_like(acc_ref)
        stats_ref[...] = jnp.zeros_like(stats_ref)
        group_row = lax.broadcasted_iota(jnp.int32, (group_rows, kept), 0)
        lane_row = lax.broadcasted_iota(jnp.int32, (LANES, kept), 0)

        def one_token(t, carry):
            ids = ids_ref[pl.ds(t, 1), :]
            high = jnp.where(group_row == (ids >> 7), 1.0, 0.0).astype(jnp.bfloat16)
            same = lane_row == (ids & 127)
            first = jnp.where(same, hi_probs_ref[pl.ds(t, 1), :], 0.0).astype(jnp.bfloat16)
            second = jnp.where(same, lo_probs_ref[pl.ds(t, 1), :], 0.0).astype(jnp.bfloat16)
            rows = lax.dot_general(
                jnp.concatenate([high, high], axis=1),
                jnp.concatenate([first, second], axis=1),
                NT, preferred_element_type=jnp.float32)
            sparse_ref[:, pl.ds(t, 1), :] = rows[:groups].reshape(groups, 1, LANES)
            return carry

        lax.fori_loop(0, tokens, one_token, 0, unroll=8)

    def block(columns):
        w = w_ref.at[pl.ds(0, columns)]
        logits = lax.dot_general(hidden_ref[...], w[...], NT, preferred_element_type=jnp.float32)
        ratio = jnp.tanh(logits * (1.0 / SOFT_CAP))
        capped = SOFT_CAP * ratio
        slope = 1.0 - ratio * ratio
        lane = lax.broadcasted_iota(jnp.int32, (tokens, columns), 1)
        exps = jnp.exp(capped)
        sparse = jnp.concatenate(
            [sparse_ref[step * (BLOCK // LANES) + i] for i in range(pl.cdiv(columns, LANES))],
            axis=1)[:, :columns]
        sparse = sparse + jnp.where(lane + step * BLOCK == targets_ref[...], CE_WEIGHT, 0.0)
        stats_ref[:, 0:1] += jnp.sum(exps, axis=1, keepdims=True)
        stats_ref[:, 1:2] += jnp.sum(capped * sparse, axis=1, keepdims=True)
        grads = jnp.concatenate([exps * slope, sparse * slope], axis=0).astype(jnp.bfloat16)
        for start in range(0, depth, ROW_CHUNK):
            part = slice(start, start + ROW_CHUNK)
            acc_ref[:, part] += jnp.dot(grads, w[:, part], preferred_element_type=jnp.float32)

    last = width - (pl.cdiv(width, BLOCK) - 1) * BLOCK

    @pl.when(step < steps - 1)
    def _():
        block(BLOCK)

    @pl.when(step == steps - 1)
    def _():
        block(last)


def head_pass(hidden, head_weight, local_ids, probs, local_targets):
    tokens, depth = hidden.shape
    width = head_weight.shape[1]
    kept = local_ids.shape[1]
    groups = pl.cdiv(width, LANES)
    hi_probs = probs.astype(jnp.bfloat16).astype(jnp.float32)
    lo_probs = probs - hi_probs
    full = lambda shape: pl.BlockSpec(shape, lambda j: (0, 0), pipeline_mode=pl.Buffered(1))
    return pl.pallas_call(
        functools.partial(head_kernel, width),
        grid=(pl.cdiv(width, BLOCK),),
        in_specs=[
            full((tokens, depth)),
            pl.BlockSpec((BLOCK, depth), lambda j: (j, 0)),
            full((tokens, kept)),
            full((tokens, kept)),
            full((tokens, kept)),
            full((tokens, 1)),
        ],
        out_specs=[full((2 * tokens, depth)), full((tokens, LANES))],
        out_shape=[
            jax.ShapeDtypeStruct((2 * tokens, depth), jnp.float32),
            jax.ShapeDtypeStruct((tokens, LANES), jnp.float32),
        ],
        scratch_shapes=[pltpu.VMEM((groups, tokens, LANES), jnp.float32)],
        compiler_params=pltpu.CompilerParams(vmem_limit_bytes=58 * 1024 * 1024),
        cost_estimate=pl.CostEstimate(
            flops=6 * tokens * depth * width, bytes_accessed=2 * depth * width,
            transcendentals=2 * tokens * width),
        name="head_pass",
    )(hidden, head_weight.T, local_ids, hi_probs, lo_probs, local_targets[:, None])


def meet(nd, nv):
    d, v = lax.axis_index("dp"), lax.axis_index("vocab")
    barrier = pltpu.get_barrier_semaphore()
    peers_v = [(d, lax.rem(v + o, nv)) for o in range(1, nv)]
    peers_d = [(lax.rem(d + o, nd), v) for o in range(1, nd)]
    for peer in peers_v + peers_d:
        pl.semaphore_signal(barrier, inc=1, device_id=peer, device_id_type=MESH)
    pl.semaphore_wait(barrier, nv + nd - 2)
    return d, v, peers_d, peers_v


def remote(src, dst, send, recv, peer):
    return pltpu.make_async_remote_copy(
        src_ref=src, dst_ref=dst, send_sem=send, recv_sem=recv,
        device_id=peer, device_id_type=MESH)


def gather_kernel(nd, nv, *refs):
    ins, outs = refs[:3], refs[3:6]
    send_v, recv_v, send_d, recv_d = refs[6:]
    d, v, peers_d, peers_v = meet(nd, nv)
    for i in range(3):
        outs[i][d * nv + v] = ins[i][...]
    copies = []
    for o, peer in enumerate(peers_v):
        for i in range(3):
            copy = remote(ins[i], outs[i].at[d * nv + v], send_v.at[i, o], recv_v.at[i, v], peer)
            copy.start()
            copies.append(copy)
    for o, peer in enumerate(peers_v):
        for i in range(3):
            source = peer[1]
            remote(ins[i], outs[i].at[d * nv + source], send_v.at[i, o],
                   recv_v.at[i, source], peer).wait_recv()
    for o, peer in enumerate(peers_d):
        for i in range(3):
            rows = outs[i].at[pl.ds(d * nv, nv)]
            copy = remote(rows, rows, send_d.at[i, o], recv_d.at[i, d], peer)
            copy.start()
            copies.append(copy)
    for o, peer in enumerate(peers_d):
        for i in range(3):
            rows = outs[i].at[pl.ds(peer[0] * nv, nv)]
            remote(rows, rows, send_d.at[i, o], recv_d.at[i, peer[0]], peer).wait_recv()
    for copy in copies:
        copy.wait_send()


def totals_kernel(nd, nv, in_ref, out_ref, slots_v, slots_d, held, send_v, recv_v, send_d, recv_d):
    d, v, peers_d, peers_v = meet(nd, nv)
    copies = []
    for peers, me, src, slots, send, recv, axis, result in (
        (peers_v, v, in_ref, slots_v, send_v, recv_v, 1, held),
        (peers_d, d, held, slots_d, send_d, recv_d, 0, out_ref),
    ):
        for o, peer in enumerate(peers):
            copy = remote(src, slots.at[me], send.at[o], recv.at[me], peer)
            copy.start()
            copies.append(copy)
        slots[me] = src[...]
        for o, peer in enumerate(peers):
            source = peer[axis]
            remote(src, slots.at[source], send.at[o], recv.at[source], peer).wait_recv()
        result[...] = jnp.sum(slots[...], axis=0)
    for copy in copies:
        copy.wait_send()


def reduce_kernel(nd, nv, in_ref, out_ref, slots_d, slots_v, held, send_d, recv_d, send_v, recv_v):
    d, v, peers_d, peers_v = meet(nd, nv)
    copies = []
    for o, peer in enumerate(peers_d):
        copy = remote(in_ref.at[peer[0]], slots_d.at[d], send_d.at[o], recv_d.at[d], peer)
        copy.start()
        copies.append(copy)
    held[...] = in_ref[d].astype(jnp.float32)
    for o, peer in enumerate(peers_d):
        source = peer[0]
        remote(in_ref.at[d], slots_d.at[source], send_d.at[o], recv_d.at[source], peer).wait_recv()
        held[...] += slots_d[source].astype(jnp.float32)
    for o, peer in enumerate(peers_v):
        copy = remote(held.at[peer[1]], slots_v.at[v], send_v.at[o], recv_v.at[v], peer)
        copy.start()
        copies.append(copy)
    total = held[v]
    for o, peer in enumerate(peers_v):
        source = peer[1]
        remote(held.at[v], slots_v.at[source], send_v.at[o], recv_v.at[source], peer).wait_recv()
        total = total + slots_v[source]
    out_ref[...] = total.astype(out_ref.dtype)
    for copy in copies:
        copy.wait_send()


def comm_call(kernel, number, name, args, out_shape, scratch):
    vmem = pl.BlockSpec(memory_space=pltpu.VMEM)
    return pl.pallas_call(
        kernel,
        out_shape=out_shape,
        in_specs=[vmem] * len(args),
        out_specs=[vmem] * len(out_shape),
        scratch_shapes=scratch,
        compiler_params=pltpu.CompilerParams(
            collective_id=number, has_side_effects=True, vmem_limit_bytes=48 * 1024 * 1024),
        name=name,
    )(*args)


def per_device(nd, nv, hidden, head_weight, teacher_ids, teacher_probs, target_ids):
    width = head_weight.shape[1]
    local_tokens, kept = teacher_ids.shape
    depth = hidden.shape[1]
    count = nd * nv
    tokens = count * local_tokens
    position = lax.axis_index(AXES)
    sems = lambda *shape: pltpu.SemaphoreType.DMA(shape)
    rows = local_tokens * depth // LANES
    pad = 8 * pl.cdiv(local_tokens + 1, 8)
    target_row = jnp.pad(target_ids, (0, kept - local_tokens))[None, :]
    ids = jnp.pad(jnp.concatenate([teacher_ids, target_row], axis=0),
                  ((0, pad - local_tokens - 1), (0, 0)))
    probs = jnp.pad(teacher_probs, ((0, pad - local_tokens), (0, 0)))
    args = (hidden.reshape(rows, LANES), ids, probs)
    got = comm_call(
        functools.partial(gather_kernel, nd, nv), 0, "gather_inputs", args,
        [jax.ShapeDtypeStruct((count,) + a.shape, a.dtype) for a in args],
        [sems(3, nv), sems(3, nv), sems(3, nd), sems(3, nd)])
    all_hidden = got[0].reshape(tokens, depth)
    local = got[1] - position * width
    local_ids = local[:, :local_tokens].reshape(tokens, kept)
    local_targets = local[:, local_tokens, :local_tokens].reshape(tokens)
    all_probs = got[2][:, :local_tokens].reshape(tokens, kept)
    acc, stats = head_pass(all_hidden, head_weight, local_ids, all_probs, local_targets)
    block = (8, tokens)
    totals = comm_call(
        functools.partial(totals_kernel, nd, nv), 1, "sum_stats", (stats[:, :8].T,),
        [jax.ShapeDtypeStruct(block, jnp.float32)],
        [pltpu.VMEM((nv,) + block, jnp.float32), pltpu.VMEM((nd,) + block, jnp.float32),
         pltpu.VMEM(block, jnp.float32), sems(nv), sems(nv), sems(nd), sems(nd)])[0]
    exp_sum, dots = totals[0], totals[1]
    teacher_sum = jnp.sum(all_probs, axis=1)
    scale = LOSS_SCALE * (teacher_sum + CE_WEIGHT) / exp_sum
    part = (scale[:, None] * acc[:tokens] - LOSS_SCALE * acc[tokens:]).astype(jnp.bfloat16)
    piece = (rows, LANES)
    grad = comm_call(
        functools.partial(reduce_kernel, nd, nv), 2, "sum_grads",
        (part.reshape((nd, nv) + piece),),
        [jax.ShapeDtypeStruct(piece, jnp.bfloat16)],
        [pltpu.VMEM((nd, nv) + piece, jnp.bfloat16), pltpu.VMEM((nv,) + piece, jnp.float32),
         pltpu.VMEM((nv,) + piece, jnp.float32), sems(nd), sems(nd), sems(nv), sems(nv)])[0]
    own = lambda x: lax.dynamic_slice_in_dim(x, position * local_tokens, local_tokens)
    own_sum = jnp.sum(teacher_probs, axis=1)
    loss = (
        jnp.sum(teacher_probs * jnp.log(teacher_probs), axis=1)
        - own(dots)
        + (own_sum + CE_WEIGHT) * jnp.log(own(exp_sum))
    )
    return loss, grad.reshape(local_tokens, depth)


def solution(mesh):
    in_specs = (
        P(AXES, None),
        P(None, AXES),
        P(AXES, None),
        P(AXES, None),
        P(AXES),
    )
    out_specs = (P(AXES), P(AXES, None))
    return jax.shard_map(
        functools.partial(per_device, mesh.shape["dp"], mesh.shape["vocab"]),
        mesh=mesh, in_specs=in_specs, out_specs=out_specs, check_vma=False
    )
```
